256 devices in a mesh: blk: 32 (over y, z), rep: 8 (over x, core).
Axes of the slice: x: 4, y: 4, z: 8, core: 2. Of those that a mesh axis runs over, the one named last changes fastest.
Arguments:
- node_feats: bfloat16 [65536, 128], P('blk'), may hold values from -6 to 6
- weight: bfloat16 [128, 256], replicated, may hold values from -0.5 to 0.5
- tile_values: bfloat16 [12288, 128, 128], P(('blk', 'rep')), may hold values from -0.109375 to 0.109375
- tile_rows: int32 [12288], P(('blk', 'rep')), may hold values from 0 to 15
- tile_cols: int32 [12288], P(('blk', 'rep')), may hold values from 0 to 511, as said below
- tile_count: int32 [256], P(('blk', 'rep')), may hold values from 12 to 48, as said below
- cotangent: bfloat16 [65536, 256], P('blk'), may hold values from -6 to 6
Outputs:
- layer_out: bfloat16 [65536, 256], P('blk')
- grad_weight: float32 [128, 256], replicated
- grad_feats: float32 [65536, 128], P(('blk', 'rep'))
The draws below stay inside these ranges and needn't reach their ends.
Inputs may be any that keep to these rules, and one draw needn't show every extreme that they name: `tile_cols`: in each tile list at most 2 slots name tile columns of one node block; in every draw one node block is named by exactly 2 slots of every list. `tile_count`: some list is full in every draw.
All inputs are finite; a program needn't handle non-finite values.
Results may differ from the reference program's by a relative error of at most 0.006.
Values may be sent and summed in bfloat16 or wider, within the bound.
A program may use at most 64 MiB of HBM per device.

```python
import math
import jax
import jax.numpy as jnp
from jax import lax

FIN = 128
HID = 256
TILE = 128
TILES_DEV = 48
TILE_ROWS = 16
NODES = 65536
COL_TILES = 512
SEND_MOST = 2
N_BLK = 32
N_REP = 8


def draw_tile_cols(key, part):
    key = jax.random.fold_in(key, 11)
    key_block, key_order, key_within = jax.random.split(key, 3)
    lists = N_BLK * N_REP
    seats = N_BLK * SEND_MOST
    common = jax.random.randint(key_block, (), 0, N_BLK, dtype=jnp.int32)
    seat_ids = jnp.arange(seats, dtype=jnp.int32)

    def one_list(list_key):
        order = jax.random.permutation(list_key, seats).astype(jnp.int32)
        score = jnp.zeros((seats,), jnp.int32).at[order].set(seat_ids)
        score = jnp.where(seat_ids // SEND_MOST == common, seat_ids - seats, score)
        return jnp.argsort(score, stable=True)[:TILES_DEV].astype(jnp.int32)
    picked = jax.vmap(one_list)(jax.random.split(key_order, lists))
    target = picked // SEND_MOST
    within = jax.random.randint(key_within, (lists, TILES_DEV), 0, TILE_ROWS, dtype=jnp.int32)
    return (target * TILE_ROWS + within).reshape(-1).astype(jnp.int32)


def draw_tile_count(key, part):
    key = jax.random.fold_in(key, 7)
    first, second = jax.random.split(key)
    lists = N_BLK * N_REP
    counts = jax.random.randint(first, (lists,), (TILES_DEV + 3) // 4, TILES_DEV + 1, dtype=jnp.int32)
    busiest = jax.random.randint(second, (), 0, lists, dtype=jnp.int32)
    return counts.at[busiest].set(TILES_DEV).astype(jnp.int32)


def touch_ends(array, stream_key, least, largest):
    longest = array.shape.index(max(array.shape))
    spots = []
    for shift in (0, 1):
        where = [jax.random.randint(jax.random.fold_in(stream_key, axis), (), 0, length) for axis, length in enumerate(array.shape)]
        where[longest] = (where[longest] + shift) % array.shape[longest]
        spots.append(tuple(where))
    return array.at[spots[0]].set(least).at[spots[1]].set(largest)


def levels(rng, dims, cuts, low, top_value):
    def one(axis_at, parts):
        heights = jax.random.uniform(jax.random.fold_in(jax.random.fold_in(rng, 6), axis_at), (parts,), jnp.float32, low / len(cuts), top_value / len(cuts))
        return jnp.repeat(jnp.exp(heights), dims[axis_at] // parts).reshape((-1,) + (1,) * (len(dims) - axis_at - 1))

    gain = one(*cuts[0])
    for cut in cuts[1:]:
        gain = gain * one(*cut)
    return gain


def normal_values(stream_key, dims, deviation, limit, cuts=(), kind=jnp.bfloat16):
    entries = jax.random.normal(stream_key, dims, jnp.float32) * deviation
    if len(cuts) > 0:
        entries = levels(stream_key, dims, cuts, -0.22, 0.18) * entries
    return jnp.clip(entries, min=-limit, max=limit).astype(kind)


def setup_inputs(seed: int = 0) -> dict:
    key_of = jax.random.split(jax.random.key(seed), 8)
    return {
        "node_feats": normal_values(key_of[0], (NODES, FIN), 1.0, 6.0, ((0, 32),)),
        "weight": normal_values(key_of[1], (FIN, HID), FIN ** -0.5, 0.5),
        "tile_values": normal_values(key_of[2], (N_BLK * N_REP * TILES_DEV, TILE, TILE), (TILE * TILES_DEV * N_REP // TILE_ROWS) ** -0.5, 0.109375, ((0, 256),)),
        "tile_rows": touch_ends(jax.random.randint(key_of[3], (N_BLK * N_REP * TILES_DEV,), 0, TILE_ROWS), jax.random.fold_in(key_of[3], 1), 0, TILE_ROWS - 1).astype(jnp.int32),
        "tile_cols": draw_tile_cols(jax.random.fold_in(key_of[7], 71), 0),
        "tile_count": draw_tile_count(jax.random.fold_in(key_of[7], 71), 0),
        "cotangent": normal_values(key_of[6], (NODES, HID), 1.0, 6.0, ((0, 32),)),
    }


def reference(node_feats, weight, tile_values, tile_rows, tile_cols, tile_count, cotangent):
    lists = N_BLK * N_REP
    values = tile_values.reshape(lists, TILES_DEV, TILE, TILE)
    rows = tile_rows.reshape(lists, TILES_DEV)
    cols = tile_cols.reshape(lists, TILES_DEV)
    owners = jnp.arange(lists, dtype=jnp.int32)
    slot = jnp.arange(TILES_DEV, dtype=jnp.int32)
    feat_tiles = node_feats.reshape(COL_TILES, TILE, FIN)

    def forward(acc, item):
        vals, row_ids, col_ids, live_count, owner = item
        live = (slot < live_count).astype(jnp.float32)
        prod = jnp.einsum('kij,kjf->kif', vals.astype(jnp.float32), feat_tiles[col_ids].astype(jnp.float32))
        target = owner // N_REP * TILE_ROWS + row_ids
        return (acc.at[target].add(prod * live[:, None, None]), None)
    total, unused = lax.scan(forward, jnp.zeros((COL_TILES, TILE, FIN), jnp.float32), (values, rows, cols, tile_count, owners))
    aggregated = total.reshape(NODES, FIN).astype(jnp.bfloat16)
    pre = jnp.dot(aggregated, weight, preferred_element_type=jnp.float32)
    layer_out = jax.nn.silu(pre).astype(jnp.bfloat16)
    sig = jax.nn.sigmoid(pre)
    dpre = (cotangent.astype(jnp.float32) * sig * (1.0 + pre * (1.0 - sig))).astype(jnp.bfloat16)
    grad_weight = jnp.dot(aggregated.T, dpre, preferred_element_type=jnp.float32) / math.sqrt(NODES)
    dagg = jnp.dot(dpre, weight.T, preferred_element_type=jnp.float32).astype(jnp.bfloat16)
    dagg_tiles = dagg.reshape(COL_TILES, TILE, FIN)

    def backward(acc, item):
        vals, row_ids, col_ids, live_count, owner = item
        live = (slot < live_count).astype(jnp.float32)
        source = owner // N_REP * TILE_ROWS + row_ids
        contrib = jnp.einsum('kji,kjf->kif', vals.astype(jnp.float32), dagg_tiles[source].astype(jnp.float32))
        return (acc.at[col_ids].add(contrib * live[:, None, None]), None)
    adjoint, unused = lax.scan(backward, jnp.zeros((COL_TILES, TILE, FIN), jnp.float32), (values, rows, cols, tile_count, owners))
    return (layer_out, grad_weight, adjoint.reshape(NODES, FIN))
```

```python
import functools
import math

import jax
import jax.numpy as jnp
from jax import lax
from jax.experimental import pallas as pl
from jax.experimental.pallas import tpu as pltpu
from jax.sharding import PartitionSpec as P

MESH = pl.DeviceIdType.MESH
BF = jnp.bfloat16
F32 = jnp.float32
NY, NZ, NX, NC = 4, 8, 4, 2
REP = NX * NC
ROWT = 16
T = 128
COPIES = 160
FWD = (0, 7, 1, 6, 2, 5, 3, 4)
BWD = (4, 3, 5, 2, 6, 1, 7, 0)


def kernel(
    feats, weight, values, meta, rq, cot,
    layer_out, grad_weight, grad_feats,
    fb0, fb1, fb2, fb3, fb4, fb5, fb6, fb7,
    sy, got, prod, acc, sb, rb, agg, dagg, gwa, gwy, gwz, gwr,
    bs, br, unp, blkp, sr, zs, zp, zm, xs, xr, half,
    send_sem, recv_sem, local_sem,
):
    blk = lax.axis_index("blk")
    rep = lax.axis_index("rep")
    y, z = blk // NZ, lax.rem(blk, NZ)
    x, c = rep // NC, lax.rem(rep, NC)
    fb = (fb0, fb1, fb2, fb3, fb4, fb5, fb6, fb7)
    used = []

    def at(yy, zz, xx, cc):
        return {"blk": yy * NZ + zz, "rep": xx * NC + cc}

    def ypeer(d):
        return at(lax.rem(y + d, NY), z, x, c)

    def zpeer(d):
        return at(y, lax.rem(z + d, NZ), x, c)

    def rpeer(d):
        return {"blk": blk, "rep": lax.rem(rep + d, REP)}

    sibling = at(y, z, x, 1 - c)

    def put(src, dst, device):
        n = len(used)
        copy = pltpu.make_async_remote_copy(
            src_ref=src, dst_ref=dst, send_sem=send_sem.at[n], recv_sem=recv_sem.at[n],
            device_id=device, device_id_type=MESH,
        )
        used.append(copy)
        copy.start()
        return copy

    own = pltpu.make_async_copy(feats, fb[0], local_sem.at[0])
    own.start()
    barrier = pltpu.get_barrier_semaphore()
    peers = (
        [ypeer(d) for d in range(1, NY)]
        + [zpeer(d) for d in range(1, NZ)]
        + [rpeer(d) for d in range(1, REP)]
    )
    for p in peers:
        pl.semaphore_signal(barrier, inc=1, device_id=p, device_id_type=MESH)
    pl.semaphore_wait(barrier, len(peers))

    own.wait()

    def chunk(j):
        return pl.ds(8 * c + 4 * j, 4)

    up, down = {}, {}
    for j in range(2):
        up[7, j] = put(fb[0].at[chunk(j)], fb[7].at[chunk(j)], zpeer(1))
        down[1, j] = put(fb[0].at[chunk(j)], fb[1].at[chunk(j)], zpeer(NZ - 1))
    shared = {}

    def arrive(e):
        for j in range(2):
            ring = up if e > 4 or (e == 4 and j == 0) else down
            ring[e, j].wait_recv()
            if e > 4 and (e > 5 or j == 0):
                up[e - 1, j] = put(fb[e].at[chunk(j)], fb[e - 1].at[chunk(j)], zpeer(1))
            if e < 4 and (e < 3 or j == 1):
                down[e + 1, j] = put(fb[e].at[chunk(j)], fb[e + 1].at[chunk(j)], zpeer(NZ - 1))
            shared[e, j] = put(fb[e].at[chunk(j)], fb[e].at[chunk(j)], sibling)

    def seat_of(d, e, k):
        return 2 * (lax.rem(y + d, NY) * NZ + lax.rem(z + e, NZ)) + k

    def ask_of(d, e, k):
        return rq[d, 2 * lax.rem(z + e, NZ) + k]

    sent = {}

    def pack(e):
        for d in range(1, NY):
            for k in range(2):
                sy[d - 1, e, k] = fb[e][ask_of(d, e, k)]
            sent[d, e] = put(sy.at[d - 1, e], got.at[NY - d, e], ypeer(d))
        for k in range(2):
            got[0, e, k] = fb[e][ask_of(0, e, k)]

    def spmm(e, first):
        for d in range(1, NY):
            sent[d, e].wait_recv()
        rows = []
        for d in range(NY):
            for k in range(2):
                seat = seat_of(d, e, k)
                prod[2 * d + k] = jnp.dot(
                    values[meta[0, seat]], got[d, e, k], preferred_element_type=F32
                )
                rows.append(meta[1, seat])

        def add(t, carry):
            total = jnp.zeros((T, T), F32) if first else acc[t]
            for i in range(2 * NY):
                total = total + prod[i] * jnp.where(rows[i] == t, 1.0, 0.0).astype(F32)
            acc[t] = total
            return carry

        lax.fori_loop(0, ROWT, add, 0)

    for i, e in enumerate(FWD):
        if e:
            arrive(e)
            if i >= 2:
                spmm(FWD[i - 2], i == 2)
            for j in range(2):
                shared[e, j].wait_recv()
        pack(e)
    spmm(FWD[-2], False)
    spmm(FWD[-1], False)

    def cast(t, carry):
        sb[t] = acc[t].astype(BF)
        return carry

    lax.fori_loop(0, ROWT, cast, 0)
    scattered = [
        put(sb.at[pl.ds(2 * lax.rem(rep + d, REP), 2)], rb.at[REP - d], rpeer(d))
        for d in range(1, REP)
    ]
    mine = acc[pl.ds(2 * rep, 2)]
    for d, copy in enumerate(scattered, 1):
        copy.wait_recv()
        mine = mine + rb[REP - d].astype(F32)
    agg[pl.ds(2 * rep, 2)] = mine.astype(BF)
    pair = agg.at[pl.ds(2 * rep, 2)]
    spread = [put(pair, pair, rpeer(d)) for d in range(1, REP)]
    for copy in spread:
        copy.wait_recv()

    gwa[...] = jnp.zeros_like(gwa)

    def dense(i, carry):
        rows = pl.ds(pl.multiple_of(i * 256, 256), 256)
        a = agg[pl.ds(2 * i, 2)].reshape(256, T)
        pre = jnp.dot(a, weight[...], preferred_element_type=F32)
        sig = jax.nn.sigmoid(pre)
        layer_out[rows, :] = (pre * sig).astype(BF)
        dpre = (cot[rows, :].astype(F32) * sig * (1.0 + pre * (1.0 - sig))).astype(BF)
        gwa[...] += lax.dot_general(a, dpre, (((0,), (0,)), ((), ())), preferred_element_type=F32)
        back = lax.dot_general(dpre, weight[...], (((1,), (1,)), ((), ())), preferred_element_type=F32)
        dagg[pl.ds(2 * i, 2)] = back.astype(BF).reshape(2, T, T)
        return carry

    lax.fori_loop(0, 8, dense, 0)

    strip = pl.ds(pl.multiple_of(16 * rep, 16), 16)
    gwy[pl.ds(y, 1)] = (gwa[strip, :] * (1.0 / 256.0))[None]
    gw_y = [put(gwy.at[pl.ds(y, 1)], gwy.at[pl.ds(y, 1)], ypeer(d)) for d in range(1, NY)]

    back_sent = {}

    def products(e):
        for d in (1, 2, 3, 0):
            for k in range(2):
                seat = seat_of(d, e, k)
                row = meta[1, seat]
                live = jnp.where(row < ROWT, 1.0, 0.0).astype(F32)
                out = lax.dot_general(
                    values[meta[0, seat]], dagg[lax.rem(row, ROWT)],
                    (((0,), (0,)), ((), ())), preferred_element_type=F32,
                )
                if d:
                    bs[d - 1, e, k] = (out * live).astype(BF)
                else:
                    br[0, e, k] = (out * live).astype(BF)
            if d:
                back_sent[d, e] = put(bs.at[d - 1, e], br.at[NY - d, e], ypeer(d))

    sib_sent = {}

    def place(t):
        return 8 * lax.rem(t // 2, 2) + 2 * (t // 4) + lax.rem(t, 2)

    def collect(e):
        ids = []
        for d in range(NY):
            if d:
                back_sent[NY - d, e].wait_recv()
            for k in range(2):
                unp[2 * d + k] = br[d, e, k].astype(F32)
                ids.append(place(ask_of(d, e, k)))

        def add(t, carry):
            total = jnp.zeros((T, T), F32)
            for i in range(2 * NY):
                total = total + unp[i] * jnp.where(ids[i] == t, 1.0, 0.0).astype(F32)
            blkp[e, t] = total.astype(BF)
            return carry

        lax.fori_loop(0, ROWT, add, 0)
        sib_sent[e] = put(blkp.at[e, pl.ds(8 * (1 - c), 8)], sr.at[e], sibling)

    zup, zdown = {}, {}

    def chain(e):
        sib_sent[e].wait_recv()
        if e == 0:
            for j in range(2):
                zup[0, j].wait_recv()
                zdown[0, j].wait_recv()

            def home(t, carry):
                half[t] = (
                    blkp[0, 8 * c + t].astype(F32) + sr[0, t].astype(F32)
                    + zp[0, t].astype(F32) + zm[0, t].astype(F32)
                )
                return carry

            lax.fori_loop(0, 8, home, 0)
            return
        for j in range(2):
            rising = e < 4 or (e == 4 and j == 0)
            begins = e == 4 or (e == 3 and j == 1) or (e == 5 and j == 0)
            if not begins:
                (zup if rising else zdown)[e, j].wait_recv()

            def step(t, carry):
                total = blkp[e, 8 * c + t].astype(F32) + sr[e, t].astype(F32)
                if not begins:
                    total = total + (zp if rising else zm)[e % 8, t].astype(F32)
                zs[e, t] = total.astype(BF)
                return carry

            lax.fori_loop(4 * j, 4 * j + 4, step, 0)
            piece = pl.ds(4 * j, 4)
            if rising:
                zup[e - 1, j] = put(zs.at[e, piece], zp.at[e - 1, piece], zpeer(1))
            else:
                zdown[(e + 1) % 8, j] = put(zs.at[e, piece], zm.at[(e + 1) % 8, piece], zpeer(NZ - 1))

    gw_z, gw_r = [], []

    def gw_second():
        for copy in gw_y:
            copy.wait_recv()
        gwz[pl.ds(z, 1)] = (gwy[0] + gwy[1] + gwy[2] + gwy[3])[None]
        for d in range(1, NZ):
            gw_z.append(put(gwz.at[pl.ds(z, 1)], gwz.at[pl.ds(z, 1)], zpeer(d)))

    def gw_third():
        for copy in gw_z:
            copy.wait_recv()
        total = gwz[0]
        for i in range(1, NZ):
            total = total + gwz[i]
        gwr[strip, :] = total
        for d in range(1, REP):
            gw_r.append(put(gwr.at[strip], gwr.at[strip], rpeer(d)))

    n = len(BWD)
    for i in range(n + 3):
        if i < n:
            products(BWD[i])
        if 2 <= i < n + 2:
            collect(BWD[i - 2])
        if 3 <= i:
            chain(BWD[i - 3])
        if i == 4:
            gw_second()
        if i == 7:
            gw_third()

    x_sent = []
    for d in range(1, NX):
        there = lax.rem(x + d, NX)
        xs[d - 1] = half[pl.ds(2 * there, 2)].astype(BF)
        x_sent.append(put(xs.at[d - 1], xr.at[NX - d], at(y, z, there, c)))
    total = half[pl.ds(2 * x, 2)]
    for copy in gw_r:
        copy.wait_recv()
    grad_weight[...] = gwr[...]
    for d, copy in enumerate(x_sent, 1):
        copy.wait_recv()
        total = total + xr[NX - d].astype(F32)
    grad_feats[...] = total.reshape(2 * T, T)
    for copy in used:
        copy.wait_send()


def body(node_feats, weight, tile_values, tile_rows, tile_cols, tile_count, cotangent):
    slots = tile_values.shape[0]
    slot = jnp.arange(slots, dtype=jnp.int32)
    live = slot < tile_count[0]
    owner = tile_cols // ROWT
    same = (owner[:, None] == owner[None, :]) & live[None, :] & (slot[None, :] < slot[:, None])
    rank = jnp.sum(same.astype(jnp.int32), axis=1)
    seat = jnp.where(live, 2 * owner + rank, -1)
    seats = 2 * NY * NZ
    hit = seat[None, :] == jnp.arange(seats, dtype=jnp.int32)[:, None]
    table = jnp.stack([slot, tile_rows - ROWT, tile_cols % ROWT])
    meta = jnp.sum(jnp.where(hit[None], table[:, None, :], 0), axis=2)
    meta = meta + jnp.array([0, ROWT, 0], jnp.int32)[:, None]
    asks = meta[2].reshape(NY, 2 * NZ)
    y = lax.axis_index("blk") // NZ
    asked = [lax.dynamic_slice_in_dim(asks, y, 1, 0)]
    for d in range(1, NY):
        row = lax.dynamic_slice_in_dim(asks, (y + NY - d) % NY, 1, 0)
        perm = [(b, (b - d * NZ) % (NY * NZ)) for b in range(NY * NZ)]
        asked.append(lax.ppermute(row, "blk", perm))
    rq = jnp.concatenate(asked, axis=0)

    vmem = pl.BlockSpec(memory_space=pltpu.VMEM)
    smem = pl.BlockSpec(memory_space=pltpu.SMEM)
    tiles = lambda *lead: pltpu.VMEM((*lead, T, T), BF)
    wide = lambda *lead: pltpu.VMEM((*lead, T, T), F32)
    outs = pl.pallas_call(
        kernel,
        out_shape=(
            jax.ShapeDtypeStruct((2048, 256), BF),
            jax.ShapeDtypeStruct((128, 256), F32),
            jax.ShapeDtypeStruct((256, 128), F32),
        ),
        in_specs=[vmem, vmem, vmem, smem, smem, vmem],
        out_specs=(vmem, vmem, vmem),
        scratch_shapes=[tiles(ROWT) for _ in range(8)] + [
            tiles(3, 8, 2), tiles(4, 8, 2), wide(8), wide(16),
            tiles(16), tiles(8, 2), tiles(16), tiles(16),
            pltpu.VMEM((128, 256), F32), pltpu.VMEM((NY, 16, 256), F32),
            pltpu.VMEM((NZ, 16, 256), F32), pltpu.VMEM((128, 256), F32),
            tiles(3, 8, 2), tiles(4, 8, 2), wide(8), tiles(8, 16), tiles(8, 8),
            tiles(8, 8), tiles(8, 8), tiles(8, 8), tiles(3, 2), tiles(4, 2), wide(8),
            pltpu.SemaphoreType.DMA((COPIES,)), pltpu.SemaphoreType.DMA((COPIES,)),
            pltpu.SemaphoreType.DMA((1,)),
        ],
        compiler_params=pltpu.CompilerParams(
            collective_id=1, has_side_effects=True, vmem_limit_bytes=56 << 20
        ),
        name="layer",
    )(node_feats.reshape(ROWT, T, T), weight, tile_values, meta[:2], rq, cotangent)
    return outs


def solution(mesh):
    in_specs = (
        P("blk", None),
        P(),
        P(("blk", "rep"), None, None),
        P(("blk", "rep")),
        P(("blk", "rep")),
        P(("blk", "rep")),
        P("blk", None),
    )
    out_specs = (P("blk", None), P(), P(("blk", "rep"), None))
    return jax.shard_map(body, mesh=mesh, in_specs=in_specs, out_specs=out_specs, check_vma=False)
```

```python
import functools
import math

import jax
import jax.numpy as jnp
from jax import lax
from jax.experimental import pallas as pl
from jax.experimental.pallas import tpu as pltpu
from jax.sharding import PartitionSpec as P

MESH = pl.DeviceIdType.MESH
BF = jnp.bfloat16
F32 = jnp.float32
NY, NZ, NX, NC = 4, 8, 4, 2
REP = NX * NC
ROWT = 16
T = 128
COPIES = 160
FWD = (0, 7, 1, 6, 2, 5, 3, 4)
BWD = (4, 3, 5, 2, 6, 1, 7, 0)


def tables(tile_cols, tile_rows, count, metav, reqv, rqv):
    n = tile_cols.shape[1]
    across = lax.broadcasted_iota(jnp.int32, (n, n), 1)
    along = lax.broadcasted_iota(jnp.int32, (n, n), 0)
    live = count[0]

    def column(row):
        square = jnp.where(across == along, jnp.broadcast_to(row, (n, n)), 0)
        return jnp.sum(square, axis=1, keepdims=True)

    cols = tile_cols[...]
    owner, within = cols >> 4, cols & 15
    owner_c = column(owner)
    same = (owner_c == jnp.broadcast_to(owner, (n, n))) & (across < along) & (across < live)
    rank = jnp.sum(jnp.where(same, 1, 0), axis=1, keepdims=True)
    slot = column(across[:1])
    seat = jnp.where(slot < live, 2 * owner_c + rank, -1)
    hit = seat == lax.broadcasted_iota(jnp.int32, (n, T), 1)

    def spread(value):
        return jnp.sum(jnp.where(hit, value, 0), axis=0, keepdims=True)

    metav[pl.ds(0, 1), :] = spread(slot)
    metav[pl.ds(1, 1), :] = spread(column(tile_rows[...]) - ROWT) + ROWT
    asks = spread(column(within))
    reqv[...] = asks
    rqv[pl.ds(0, 1), :] = asks


def kernel(
    feats, weight, tile_values, tile_cols, tile_rows, count, cotangent,
    layer_out, grad_weight, grad_feats,
    fb0, fb1, fb2, fb3, fb4, fb5, fb6, fb7,
    values, cot, lo, metav, meta, reqv, rqv, rq,
    sy, got, prod, acc, sb, rb, agg, dagg, gwa, gwy, gwz, gwr,
    bs, br, unp, blkp, sr, zs, zp, zm, xs, xr, half,
    send_sem, recv_sem, local_sem,
):
    blk = lax.axis_index("blk")
    rep = lax.axis_index("rep")
    y, z = blk // NZ, lax.rem(blk, NZ)
    x, c = rep // NC, lax.rem(rep, NC)
    fb = (fb0, fb1, fb2, fb3, fb4, fb5, fb6, fb7)
    used = []

    def at(yy, zz, xx, cc):
        return {"blk": yy * NZ + zz, "rep": xx * NC + cc}

    def ypeer(d):
        return at(lax.rem(y + d, NY), z, x, c)

    def zpeer(d):
        return at(y, lax.rem(z + d, NZ), x, c)

    def rpeer(d):
        return {"blk": blk, "rep": lax.rem(rep + d, REP)}

    sibling = at(y, z, x, 1 - c)

    def put(src, dst, device):
        n = len(used)
        copy = pltpu.make_async_remote_copy(
            src_ref=src, dst_ref=dst, send_sem=send_sem.at[n], recv_sem=recv_sem.at[n],
            device_id=device, device_id_type=MESH,
        )
        used.append(copy)
        copy.start()
        return copy

    own = pltpu.make_async_copy(feats, fb[0], local_sem.at[0])
    load_values = pltpu.make_async_copy(tile_values, values, local_sem.at[1])
    load_cot = pltpu.make_async_copy(cotangent, cot, local_sem.at[2])
    load_meta = pltpu.make_async_copy(metav, meta, local_sem.at[3])
    load_rq = pltpu.make_async_copy(rqv, rq, local_sem.at[4])
    store_lo = pltpu.make_async_copy(lo, layer_out, local_sem.at[5])
    barrier = pltpu.get_barrier_semaphore()
    peers = (
        [ypeer(d) for d in range(1, NY)]
        + [zpeer(d) for d in range(1, NZ)]
        + [rpeer(d) for d in range(1, REP)]
    )
    for p in peers:
        pl.semaphore_signal(barrier, inc=1, device_id=p, device_id_type=MESH)
    own.start()
    load_values.start()
    load_cot.start()
    tables(tile_cols, tile_rows, count, metav, reqv, rqv)
    load_meta.start()
    pl.semaphore_wait(barrier, len(peers))

    asked = [put(reqv, rqv.at[pl.ds(NY - d, 1)], ypeer(d)) for d in range(1, NY)]

    own.wait()

    def chunk(j):
        return pl.ds(8 * c + 4 * j, 4)

    up, down = {}, {}
    for j in range(2):
        up[7, j] = put(fb[0].at[chunk(j)], fb[7].at[chunk(j)], zpeer(1))
        down[1, j] = put(fb[0].at[chunk(j)], fb[1].at[chunk(j)], zpeer(NZ - 1))
    shared = {}

    def arrive(e):
        for j in range(2):
            ring = up if e > 4 or (e == 4 and j == 0) else down
            ring[e, j].wait_recv()
            if e > 4 and (e > 5 or j == 0):
                up[e - 1, j] = put(fb[e].at[chunk(j)], fb[e - 1].at[chunk(j)], zpeer(1))
            if e < 4 and (e < 3 or j == 1):
                down[e + 1, j] = put(fb[e].at[chunk(j)], fb[e + 1].at[chunk(j)], zpeer(NZ - 1))
            shared[e, j] = put(fb[e].at[chunk(j)], fb[e].at[chunk(j)], sibling)

    def seat_of(d, e, k):
        return 2 * (lax.rem(y + d, NY) * NZ + lax.rem(z + e, NZ)) + k

    def ask_of(d, e, k):
        return rq[d, seat_of(0, e, k)] & (ROWT - 1)

    def slot_in(seat):
        return jnp.clip(meta[0, seat], 0, values.shape[0] - 1)

    sent = {}

    def pack(e):
        for d in range(1, NY):
            for k in range(2):
                sy[d - 1, e, k] = fb[e][ask_of(d, e, k)]
            sent[d, e] = put(sy.at[d - 1, e], got.at[NY - d, e], ypeer(d))
        for k in range(2):
            got[0, e, k] = fb[e][ask_of(0, e, k)]

    def spmm(e, first):
        for d in range(1, NY):
            sent[d, e].wait_recv()
        rows = []
        for d in range(NY):
            for k in range(2):
                seat = seat_of(d, e, k)
                prod[2 * d + k] = jnp.dot(
                    values[slot_in(seat)], got[d, e, k], preferred_element_type=F32
                )
                rows.append(meta[1, seat])

        def add(t, carry):
            total = jnp.zeros((T, T), F32) if first else acc[t]
            for i in range(2 * NY):
                total = total + prod[i] * jnp.where(rows[i] == t, 1.0, 0.0).astype(F32)
            acc[t] = total
            return carry

        lax.fori_loop(0, ROWT, add, 0)

    for i, e in enumerate(FWD):
        if e:
            arrive(e)
            if i >= 2:
                spmm(FWD[i - 2], i == 2)
            for j in range(2):
                shared[e, j].wait_recv()
        else:
            for copy in asked:
                copy.wait_recv()
            load_rq.start()
            load_meta.wait()
            load_values.wait()
            load_rq.wait()
        pack(e)
    spmm(FWD[-2], False)
    spmm(FWD[-1], False)

    def cast(t, carry):
        sb[t] = acc[t].astype(BF)
        return carry

    lax.fori_loop(0, ROWT, cast, 0)
    scattered = [
        put(sb.at[pl.ds(2 * lax.rem(rep + d, REP), 2)], rb.at[REP - d], rpeer(d))
        for d in range(1, REP)
    ]
    mine = acc[pl.ds(2 * rep, 2)]
    for d, copy in enumerate(scattered, 1):
        copy.wait_recv()
        mine = mine + rb[REP - d].astype(F32)
    agg[pl.ds(2 * rep, 2)] = mine.astype(BF)
    pair = agg.at[pl.ds(2 * rep, 2)]
    spread = [put(pair, pair, rpeer(d)) for d in range(1, REP)]
    for copy in spread:
        copy.wait_recv()

    gwa[...] = jnp.zeros_like(gwa)
    load_cot.wait()

    def dense(i, carry):
        rows = pl.ds(pl.multiple_of(i * 256, 256), 256)
        a = agg[pl.ds(2 * i, 2)].reshape(256, T)
        pre = jnp.dot(a, weight[...], preferred_element_type=F32)
        sig = jax.nn.sigmoid(pre)
        lo[rows, :] = (pre * sig).astype(BF)
        dpre = (cot[rows, :].astype(F32) * sig * (1.0 + pre * (1.0 - sig))).astype(BF)
        gwa[...] += lax.dot_general(a, dpre, (((0,), (0,)), ((), ())), preferred_element_type=F32)
        back = lax.dot_general(dpre, weight[...], (((1,), (1,)), ((), ())), preferred_element_type=F32)
        dagg[pl.ds(2 * i, 2)] = back.astype(BF).reshape(2, T, T)
        return carry

    lax.fori_loop(0, 8, dense, 0)
    store_lo.start()

    strip = pl.ds(pl.multiple_of(16 * rep, 16), 16)
    gwy[pl.ds(y, 1)] = (gwa[strip, :] * (1.0 / 256.0))[None]
    gw_y = [put(gwy.at[pl.ds(y, 1)], gwy.at[pl.ds(y, 1)], ypeer(d)) for d in range(1, NY)]

    back_sent = {}

    def products(e):
        for d in (1, 2, 3, 0):
            for k in range(2):
                seat = seat_of(d, e, k)
                row = meta[1, seat]
                live = jnp.where(row < ROWT, 1.0, 0.0).astype(F32)
                out = lax.dot_general(
                    values[slot_in(seat)], dagg[row & (ROWT - 1)],
                    (((0,), (0,)), ((), ())), preferred_element_type=F32,
                )
                if d:
                    bs[d - 1, e, k] = (out * live).astype(BF)
                else:
                    br[0, e, k] = (out * live).astype(BF)
            if d:
                back_sent[d, e] = put(bs.at[d - 1, e], br.at[NY - d, e], ypeer(d))

    sib_sent = {}

    def place(t):
        return 8 * lax.rem(t // 2, 2) + 2 * (t // 4) + lax.rem(t, 2)

    def collect(e):
        ids = []
        for d in range(NY):
            if d:
                back_sent[NY - d, e].wait_recv()
            for k in range(2):
                unp[2 * d + k] = br[d, e, k].astype(F32)
                ids.append(place(ask_of(d, e, k)))

        def add(t, carry):
            total = jnp.zeros((T, T), F32)
            for i in range(2 * NY):
                total = total + unp[i] * jnp.where(ids[i] == t, 1.0, 0.0).astype(F32)
            blkp[e, t] = total.astype(BF)
            return carry

        lax.fori_loop(0, ROWT, add, 0)
        sib_sent[e] = put(blkp.at[e, pl.ds(8 * (1 - c), 8)], sr.at[e], sibling)

    zup, zdown = {}, {}

    def chain(e):
        sib_sent[e].wait_recv()
        if e == 0:
            for j in range(2):
                zup[0, j].wait_recv()
                zdown[0, j].wait_recv()

            def home(t, carry):
                half[t] = (
                    blkp[0, 8 * c + t].astype(F32) + sr[0, t].astype(F32)
                    + zp[0, t].astype(F32) + zm[0, t].astype(F32)
                )
                return carry

            lax.fori_loop(0, 8, home, 0)
            return
        for j in range(2):
            rising = e < 4 or (e == 4 and j == 0)
            begins = e == 4 or (e == 3 and j == 1) or (e == 5 and j == 0)
            if not begins:
                (zup if rising else zdown)[e, j].wait_recv()

            def step(t, carry):
                total = blkp[e, 8 * c + t].astype(F32) + sr[e, t].astype(F32)
                if not begins:
                    total = total + (zp if rising else zm)[e % 8, t].astype(F32)
                zs[e, t] = total.astype(BF)
                return carry

            lax.fori_loop(4 * j, 4 * j + 4, step, 0)
            piece = pl.ds(4 * j, 4)
            if rising:
                zup[e - 1, j] = put(zs.at[e, piece], zp.at[e - 1, piece], zpeer(1))
            else:
                zdown[(e + 1) % 8, j] = put(zs.at[e, piece], zm.at[(e + 1) % 8, piece], zpeer(NZ - 1))

    gw_z, gw_r = [], []

    def gw_second():
        for copy in gw_y:
            copy.wait_recv()
        gwz[pl.ds(z, 1)] = (gwy[0] + gwy[1] + gwy[2] + gwy[3])[None]
        for d in range(1, NZ):
            gw_z.append(put(gwz.at[pl.ds(z, 1)], gwz.at[pl.ds(z, 1)], zpeer(d)))

    def gw_third():
        for copy in gw_z:
            copy.wait_recv()
        total = gwz[0]
        for i in range(1, NZ):
            total = total + gwz[i]
        gwr[strip, :] = total
        for d in range(1, REP):
            gw_r.append(put(gwr.at[strip], gwr.at[strip], rpeer(d)))

    n = len(BWD)
    for i in range(n + 3):
        if i < n:
            products(BWD[i])
        if 2 <= i < n + 2:
            collect(BWD[i - 2])
        if 3 <= i:
            chain(BWD[i - 3])
        if i == 4:
            gw_second()
        if i == 7:
            gw_third()

    x_sent = []
    for d in range(1, NX):
        there = lax.rem(x + d, NX)
        xs[d - 1] = half[pl.ds(2 * there, 2)].astype(BF)
        x_sent.append(put(xs.at[d - 1], xr.at[NX - d], at(y, z, there, c)))
    total = half[pl.ds(2 * x, 2)]
    for copy in gw_r:
        copy.wait_recv()
    grad_weight[...] = gwr[...]
    for d, copy in enumerate(x_sent, 1):
        copy.wait_recv()
        total = total + xr[NX - d].astype(F32)
    grad_feats[...] = total.reshape(2 * T, T)
    store_lo.wait()
    for copy in used:
        copy.wait_send()


def body(node_feats, weight, tile_values, tile_rows, tile_cols, tile_count, cotangent):
    slots = tile_values.shape[0]
    vmem = pl.BlockSpec(memory_space=pltpu.VMEM)
    smem = pl.BlockSpec(memory_space=pltpu.SMEM)
    hbm = pl.BlockSpec(memory_space=pl.ANY)
    ints = lambda space, n: space((n, T), jnp.int32)
    tiles = lambda *lead: pltpu.VMEM((*lead, T, T), BF)
    wide = lambda *lead: pltpu.VMEM((*lead, T, T), F32)
    outs = pl.pallas_call(
        kernel,
        out_shape=(
            jax.ShapeDtypeStruct((2048, 256), BF),
            jax.ShapeDtypeStruct((128, 256), F32),
            jax.ShapeDtypeStruct((256, 128), F32),
        ),
        in_specs=[hbm, vmem, hbm, vmem, vmem, smem, hbm],
        out_specs=(hbm, vmem, vmem),
        scratch_shapes=[tiles(ROWT) for _ in range(8)] + [
            tiles(slots), pltpu.VMEM((2048, 256), BF), pltpu.VMEM((2048, 256), BF),
            ints(pltpu.VMEM, 2), ints(pltpu.SMEM, 2), ints(pltpu.VMEM, 1),
            ints(pltpu.VMEM, 4), ints(pltpu.SMEM, 4),
            tiles(3, 8, 2), tiles(4, 8, 2), wide(8), wide(16),
            tiles(16), tiles(8, 2), tiles(16), tiles(16),
            pltpu.VMEM((128, 256), F32), pltpu.VMEM((NY, 16, 256), F32),
            pltpu.VMEM((NZ, 16, 256), F32), pltpu.VMEM((128, 256), F32),
            tiles(3, 8, 2), tiles(4, 8, 2), wide(8), tiles(8, 16), tiles(8, 8),
            tiles(8, 8), tiles(8, 8), tiles(8, 8), tiles(3, 2), tiles(4, 2), wide(8),
            pltpu.SemaphoreType.DMA((COPIES,)), pltpu.SemaphoreType.DMA((COPIES,)),
            pltpu.SemaphoreType.DMA((6,)),
        ],
        compiler_params=pltpu.CompilerParams(
            collective_id=1, has_side_effects=True, vmem_limit_bytes=56 << 20
        ),
        name="layer",
    )(node_feats.reshape(ROWT, T, T), weight, tile_values,
      tile_cols.reshape(1, slots), tile_rows.reshape(1, slots), tile_count, cotangent)
    return outs


def solution(mesh):
    in_specs = (
        P("blk", None),
        P(),
        P(("blk", "rep"), None, None),
        P(("blk", "rep")),
        P(("blk", "rep")),
        P(("blk", "rep")),
        P("blk", None),
    )
    out_specs = (P("blk", None), P(), P(("blk", "rep"), None))
    return jax.shard_map(body, mesh=mesh, in_specs=in_specs, out_specs=out_specs, check_vma=False)
```

```python
import functools
import math

import jax
import jax.numpy as jnp
from jax import lax
from jax.experimental import pallas as pl
from jax.experimental.pallas import tpu as pltpu
from jax.sharding import PartitionSpec as P

MESH = pl.DeviceIdType.MESH
BF = jnp.bfloat16
F32 = jnp.float32
NY, NZ, NX, NC = 4, 8, 4, 2
REP = NX * NC
ROWT = 16
T = 128
COPIES = 160
FWD = (0, 7, 1, 6, 2, 5, 3, 4)
BWD = (4, 3, 5, 2, 6, 1, 7, 0)


def tables(tile_cols, tile_rows, count, metav, reqv, rqv):
    n = tile_cols.shape[1]
    across = lax.broadcasted_iota(jnp.int32, (n, n), 1)
    along = lax.broadcasted_iota(jnp.int32, (n, n), 0)
    live = count[0]

    def column(row):
        square = jnp.where(across == along, jnp.broadcast_to(row, (n, n)), 0)
        return jnp.sum(square, axis=1, keepdims=True)

    cols = tile_cols[...]
    owner, within = cols >> 4, cols & 15
    owner_c = column(owner)
    same = (owner_c == jnp.broadcast_to(owner, (n, n))) & (across < along) & (across < live)
    rank = jnp.sum(jnp.where(same, 1, 0), axis=1, keepdims=True)
    slot = column(across[:1])
    seat = jnp.where(slot < live, 2 * owner_c + rank, -1)
    hit = seat == lax.broadcasted_iota(jnp.int32, (n, T), 1)

    def spread(value):
        return jnp.sum(jnp.where(hit, value, 0), axis=0, keepdims=True)

    metav[pl.ds(0, 1), :] = spread(slot)
    metav[pl.ds(1, 1), :] = spread(column(tile_rows[...]) - ROWT) + ROWT
    asks = spread(column(within))
    reqv[...] = asks
    rqv[pl.ds(0, 1), :] = asks


def kernel(
    feats, weight, tile_values, tile_cols, tile_rows, count, cotangent,
    layer_out, grad_weight, grad_feats,
    fb0, fb1, fb2, fb3, fb4, fb5, fb6, fb7,
    values, cot, lo, metav, meta, reqv, rqv, rq,
    sy, got, prod, acc, sb, rb, fxs, fxr, mine, agg, dagg, gwa, gwy, gwz, gwr,
    bs, br, unp, blkp, sr, zs, zp, zm, xs, xr, half,
    send_sem, recv_sem, local_sem,
):
    blk = lax.axis_index("blk")
    rep = lax.axis_index("rep")
    y, z = blk // NZ, lax.rem(blk, NZ)
    x, c = rep // NC, lax.rem(rep, NC)
    fb = (fb0, fb1, fb2, fb3, fb4, fb5, fb6, fb7)
    used = []

    def at(yy, zz, xx, cc):
        return {"blk": yy * NZ + zz, "rep": xx * NC + cc}

    def ypeer(d):
        return at(lax.rem(y + d, NY), z, x, c)

    def zpeer(d):
        return at(y, lax.rem(z + d, NZ), x, c)

    def rpeer(d):
        return {"blk": blk, "rep": lax.rem(rep + d, REP)}

    sibling = at(y, z, x, 1 - c)

    def put(src, dst, device):
        n = len(used)
        copy = pltpu.make_async_remote_copy(
            src_ref=src, dst_ref=dst, send_sem=send_sem.at[n], recv_sem=recv_sem.at[n],
            device_id=device, device_id_type=MESH,
        )
        used.append(copy)
        copy.start()
        return copy

    own = pltpu.make_async_copy(feats, fb[0], local_sem.at[0])
    load_values = pltpu.make_async_copy(tile_values, values, local_sem.at[1])
    load_cot = pltpu.make_async_copy(cotangent, cot, local_sem.at[2])
    load_meta = pltpu.make_async_copy(metav, meta, local_sem.at[3])
    load_rq = pltpu.make_async_copy(rqv, rq, local_sem.at[4])
    store_lo = pltpu.make_async_copy(lo, layer_out, local_sem.at[5])
    barrier = pltpu.get_barrier_semaphore()
    peers = (
        [ypeer(d) for d in range(1, NY)]
        + [zpeer(d) for d in range(1, NZ)]
        + [rpeer(d) for d in range(1, REP)]
    )
    for p in peers:
        pl.semaphore_signal(barrier, inc=1, device_id=p, device_id_type=MESH)
    own.start()
    load_values.start()
    load_cot.start()
    tables(tile_cols, tile_rows, count, metav, reqv, rqv)
    load_meta.start()
    pl.semaphore_wait(barrier, len(peers))

    asked = [put(reqv, rqv.at[pl.ds(NY - d, 1)], ypeer(d)) for d in range(1, NY)]

    own.wait()

    def chunk(j):
        return pl.ds(8 * c + 4 * j, 4)

    up, down = {}, {}
    for j in range(2):
        up[7, j] = put(fb[0].at[chunk(j)], fb[7].at[chunk(j)], zpeer(1))
        down[1, j] = put(fb[0].at[chunk(j)], fb[1].at[chunk(j)], zpeer(NZ - 1))
    shared = {}

    def arrive(e):
        for j in range(2):
            ring = up if e > 4 or (e == 4 and j == 0) else down
            ring[e, j].wait_recv()
            if e > 4 and (e > 5 or j == 0):
                up[e - 1, j] = put(fb[e].at[chunk(j)], fb[e - 1].at[chunk(j)], zpeer(1))
            if e < 4 and (e < 3 or j == 1):
                down[e + 1, j] = put(fb[e].at[chunk(j)], fb[e + 1].at[chunk(j)], zpeer(NZ - 1))
            shared[e, j] = put(fb[e].at[chunk(j)], fb[e].at[chunk(j)], sibling)

    def seat_of(d, e, k):
        return 2 * (lax.rem(y + d, NY) * NZ + lax.rem(z + e, NZ)) + k

    def ask_of(d, e, k):
        return rq[d, seat_of(0, e, k)] & (ROWT - 1)

    def slot_in(seat):
        return jnp.clip(meta[0, seat], 0, values.shape[0] - 1)

    sent = {}

    def pack(e):
        for d in range(1, NY):
            for k in range(2):
                sy[d - 1, e, k] = fb[e][ask_of(d, e, k)]
            sent[d, e] = put(sy.at[d - 1, e], got.at[NY - d, e], ypeer(d))
        for k in range(2):
            got[0, e, k] = fb[e][ask_of(0, e, k)]

    def spmm(e, first):
        for d in range(1, NY):
            sent[d, e].wait_recv()
        rows = []
        for d in range(NY):
            for k in range(2):
                seat = seat_of(d, e, k)
                prod[2 * d + k] = jnp.dot(
                    values[slot_in(seat)], got[d, e, k], preferred_element_type=F32
                )
                rows.append(meta[1, seat])

        def add(t, carry):
            total = jnp.zeros((T, T), F32) if first else acc[t]
            for i in range(2 * NY):
                total = total + prod[i] * jnp.where(rows[i] == t, 1.0, 0.0).astype(F32)
            acc[t] = total
            return carry

        lax.fori_loop(0, ROWT, add, 0)

    for i, e in enumerate(FWD):
        if e:
            arrive(e)
            if i >= 2:
                spmm(FWD[i - 2], i == 2)
            for j in range(2):
                shared[e, j].wait_recv()
        else:
            for copy in asked:
                copy.wait_recv()
            load_rq.start()
            load_meta.wait()
            load_values.wait()
            load_rq.wait()
        pack(e)
    spmm(FWD[-2], False)
    spmm(FWD[-1], False)

    def home_tile(there, j):
        return 4 * there + 2 * c + j

    def other_tile(there, j):
        return 4 * there + 2 * (1 - c) + j

    order = [lax.rem(x + d, NX) for d in (2, 1, 3, 0)]
    halves = []
    for q, there in enumerate(order):
        for j in range(2):
            sb[q, j] = acc[other_tile(there, j)].astype(BF)
        halves.append(put(sb.at[q], rb.at[q], sibling))
    scattered = {}
    for q, there in enumerate(order):
        halves[q].wait_recv()
        for j in range(2):
            total = acc[home_tile(there, j)] + rb[q, j].astype(F32)
            if q < 3:
                fxs[q, j] = total.astype(BF)
            else:
                mine[j] = total
        if q < 3:
            d = (2, 1, 3)[q]
            scattered[d] = put(fxs.at[q], fxr.at[NX - d], at(y, z, there, c))
    for d in (1, 3, 2):
        scattered[NX - d].wait_recv()
        for j in range(2):
            mine[j] += fxr[d, j].astype(F32)
    own_pair = pl.ds(2 * rep, 2)
    own_rows = pl.ds(pl.multiple_of(256 * rep, 256), 256)

    def slope(a, cots):
        pre = jnp.dot(a, weight[...], preferred_element_type=F32)
        sig = jax.nn.sigmoid(pre)
        dpre = (cots.astype(F32) * sig * (1.0 + pre * (1.0 - sig))).astype(BF)
        return pre, sig, dpre

    load_cot.wait()
    agg[own_pair] = mine[...].astype(BF)
    _, _, dpre_own = slope(mine[...].astype(BF).reshape(256, T), cot[own_rows, :])
    back = lax.dot_general(dpre_own, weight[...], (((1,), (1,)), ((), ())), preferred_element_type=F32)
    dagg[own_pair] = back.astype(BF).reshape(2, T, T)

    def pair_of(xx, cc):
        return pl.ds(2 * (2 * xx + cc), 2)

    gathered = {d: put(dagg.at[own_pair], dagg.at[own_pair], at(y, z, lax.rem(x + d, NX), c)) for d in (2, 1, 3)}
    passed = [put(dagg.at[own_pair], dagg.at[own_pair], sibling)]
    for d in (1, 3, 2):
        gathered[d].wait_recv()
        piece = dagg.at[pair_of(lax.rem(x + NX - d, NX), c)]
        passed.append(put(piece, piece, sibling))
    for copy in passed:
        copy.wait_recv()
    agg_all = [put(agg.at[own_pair], agg.at[own_pair], rpeer(d)) for d in range(1, REP)]

    gwa[...] = jnp.zeros_like(gwa)

    def dense(i, carry):
        rows = pl.ds(pl.multiple_of(i * 256, 256), 256)
        a = agg[pl.ds(2 * i, 2)].reshape(256, T)
        pre, sig, dpre = slope(a, cot[rows, :])
        lo[rows, :] = (pre * sig).astype(BF)
        gwa[...] += lax.dot_general(a, dpre, (((0,), (0,)), ((), ())), preferred_element_type=F32)
        return carry

    strip = pl.ds(pl.multiple_of(16 * rep, 16), 16)
    gw_y = []

    def gw_first():
        gwy[pl.ds(y, 1)] = (gwa[strip, :] * (1.0 / 256.0))[None]
        for d in range(1, NY):
            gw_y.append(put(gwy.at[pl.ds(y, 1)], gwy.at[pl.ds(y, 1)], ypeer(d)))

    back_sent = {}

    def products(e):
        for d in (1, 2, 3, 0):
            for k in range(2):
                seat = seat_of(d, e, k)
                row = meta[1, seat]
                live = jnp.where(row < ROWT, 1.0, 0.0).astype(F32)
                out = lax.dot_general(
                    values[slot_in(seat)], dagg[row & (ROWT - 1)],
                    (((0,), (0,)), ((), ())), preferred_element_type=F32,
                )
                if d:
                    bs[d - 1, e, k] = (out * live).astype(BF)
                else:
                    br[0, e, k] = (out * live).astype(BF)
            if d:
                back_sent[d, e] = put(bs.at[d - 1, e], br.at[NY - d, e], ypeer(d))

    sib_sent = {}

    def place(t):
        return 8 * lax.rem(t // 2, 2) + 2 * (t // 4) + lax.rem(t, 2)

    def collect(e):
        ids = []
        for d in range(NY):
            if d:
                back_sent[NY - d, e].wait_recv()
            for k in range(2):
                unp[2 * d + k] = br[d, e, k].astype(F32)
                ids.append(place(ask_of(d, e, k)))

        def add(t, carry):
            total = jnp.zeros((T, T), F32)
            for i in range(2 * NY):
                total = total + unp[i] * jnp.where(ids[i] == t, 1.0, 0.0).astype(F32)
            blkp[e, t] = total.astype(BF)
            return carry

        lax.fori_loop(0, ROWT, add, 0)
        sib_sent[e] = put(blkp.at[e, pl.ds(8 * (1 - c), 8)], sr.at[e], sibling)

    zup, zdown = {}, {}

    def chain(e):
        sib_sent[e].wait_recv()
        if e == 0:
            for j in range(2):
                zup[0, j].wait_recv()
                zdown[0, j].wait_recv()

            def home(t, carry):
                half[t] = (
                    blkp[0, 8 * c + t].astype(F32) + sr[0, t].astype(F32)
                    + zp[0, t].astype(F32) + zm[0, t].astype(F32)
                )
                return carry

            lax.fori_loop(0, 8, home, 0)
            return
        for j in range(2):
            rising = e < 4 or (e == 4 and j == 0)
            begins = e == 4 or (e == 3 and j == 1) or (e == 5 and j == 0)
            if not begins:
                (zup if rising else zdown)[e, j].wait_recv()

            def step(t, carry):
                total = blkp[e, 8 * c + t].astype(F32) + sr[e, t].astype(F32)
                if not begins:
                    total = total + (zp if rising else zm)[e % 8, t].astype(F32)
                zs[e, t] = total.astype(BF)
                return carry

            lax.fori_loop(4 * j, 4 * j + 4, step, 0)
            piece = pl.ds(4 * j, 4)
            if rising:
                zup[e - 1, j] = put(zs.at[e, piece], zp.at[e - 1, piece], zpeer(1))
            else:
                zdown[(e + 1) % 8, j] = put(zs.at[e, piece], zm.at[(e + 1) % 8, piece], zpeer(NZ - 1))

    gw_z, gw_r = [], []

    def gw_second():
        for copy in gw_y:
            copy.wait_recv()
        gwz[pl.ds(z, 1)] = (gwy[0] + gwy[1] + gwy[2] + gwy[3])[None]
        for d in range(1, NZ):
            gw_z.append(put(gwz.at[pl.ds(z, 1)], gwz.at[pl.ds(z, 1)], zpeer(d)))

    def gw_third():
        for copy in gw_z:
            copy.wait_recv()
        total = gwz[0]
        for i in range(1, NZ):
            total = total + gwz[i]
        gwr[strip, :] = total
        for d in range(1, REP):
            gw_r.append(put(gwr.at[strip], gwr.at[strip], rpeer(d)))

    n = len(BWD)
    for i in range(n + 3):
        if i < n:
            products(BWD[i])
        if 2 <= i < n + 2:
            collect(BWD[i - 2])
        if 3 <= i:
            chain(BWD[i - 3])
        if i == 2:
            for copy in agg_all:
                copy.wait_recv()
        if 2 <= i < 6:
            lax.fori_loop(2 * i - 4, 2 * i - 2, dense, 0)
        if i == 5:
            store_lo.start()
            gw_first()
        if i == 7:
            gw_second()
        if i == 9:
            gw_third()

    x_sent = []
    for d in range(1, NX):
        there = lax.rem(x + d, NX)
        xs[d - 1] = half[pl.ds(2 * there, 2)].astype(BF)
        x_sent.append(put(xs.at[d - 1], xr.at[NX - d], at(y, z, there, c)))
    total = half[pl.ds(2 * x, 2)]
    for copy in gw_r:
        copy.wait_recv()
    grad_weight[...] = gwr[...]
    for d, copy in enumerate(x_sent, 1):
        copy.wait_recv()
        total = total + xr[NX - d].astype(F32)
    grad_feats[...] = total.reshape(2 * T, T)
    store_lo.wait()
    for copy in used:
        copy.wait_send()


def finish(lo, gw, gf, lo_out, gw_out, gf_out, lo_v, gw_v, gf_v, sems):
    parts = [(lo.at[pl.ds(512 * i, 512)], lo_v.at[pl.ds(512 * i, 512)], lo_out.at[pl.ds(512 * i, 512)]) for i in range(4)]
    parts += [(gw, gw_v, gw_out), (gf, gf_v, gf_out)]
    loads = [pltpu.make_async_copy(a, v, sems.at[0, i]) for i, (a, v, _) in enumerate(parts)]
    stores = [pltpu.make_async_copy(v, o, sems.at[1, i]) for i, (_, v, o) in enumerate(parts)]
    for copy in loads:
        copy.start()
    for load, store in zip(loads, stores):
        load.wait()
        store.start()
    for copy in stores:
        copy.wait()


def body(node_feats, weight, tile_values, tile_rows, tile_cols, tile_count, cotangent):
    slots = tile_values.shape[0]
    vmem = pl.BlockSpec(memory_space=pltpu.VMEM)
    smem = pl.BlockSpec(memory_space=pltpu.SMEM)
    hbm = pl.BlockSpec(memory_space=pl.ANY)
    ints = lambda space, n: space((n, T), jnp.int32)
    tiles = lambda *lead: pltpu.VMEM((*lead, T, T), BF)
    wide = lambda *lead: pltpu.VMEM((*lead, T, T), F32)
    outs = pl.pallas_call(
        kernel,
        out_shape=(
            jax.ShapeDtypeStruct((2048, 256), BF),
            jax.ShapeDtypeStruct((128, 256), F32),
            jax.ShapeDtypeStruct((256, 128), F32),
        ),
        in_specs=[hbm, vmem, hbm, vmem, vmem, smem, hbm],
        out_specs=(hbm, vmem, vmem),
        scratch_shapes=[tiles(ROWT) for _ in range(8)] + [
            tiles(slots), pltpu.VMEM((2048, 256), BF), pltpu.VMEM((2048, 256), BF),
            ints(pltpu.VMEM, 2), ints(pltpu.SMEM, 2), ints(pltpu.VMEM, 1),
            ints(pltpu.VMEM, 4), ints(pltpu.SMEM, 4),
            tiles(3, 8, 2), tiles(4, 8, 2), wide(8), wide(16),
            tiles(4, 2), tiles(4, 2), tiles(3, 2), tiles(4, 2), wide(2), tiles(16), tiles(16),
            pltpu.VMEM((128, 256), F32), pltpu.VMEM((NY, 16, 256), F32),
            pltpu.VMEM((NZ, 16, 256), F32), pltpu.VMEM((128, 256), F32),
            tiles(3, 8, 2), tiles(4, 8, 2), wide(8), tiles(8, 16), tiles(8, 8),
            tiles(8, 8), tiles(8, 8), tiles(8, 8), tiles(3, 2), tiles(4, 2), wide(8),
            pltpu.SemaphoreType.DMA((COPIES,)), pltpu.SemaphoreType.DMA((COPIES,)),
            pltpu.SemaphoreType.DMA((6,)),
        ],
        compiler_params=pltpu.CompilerParams(
            collective_id=1, has_side_effects=True, vmem_limit_bytes=56 << 20
        ),
        name="layer",
    )(node_feats.reshape(ROWT, T, T), weight, tile_values,
      tile_cols.reshape(1, slots), tile_rows.reshape(1, slots), tile_count, cotangent)
    return pl.pallas_call(
        finish,
        out_shape=tuple(jax.ShapeDtypeStruct(o.shape, o.dtype) for o in outs),
        in_specs=[hbm] * 3,
        out_specs=(hbm,) * 3,
        scratch_shapes=[pltpu.VMEM(o.shape, o.dtype) for o in outs] + [pltpu.SemaphoreType.DMA((2, 6))],
        name="finish",
    )(*outs)


def solution(mesh):
    in_specs = (
        P("blk", None),
        P(),
        P(("blk", "rep"), None, None),
        P(("blk", "rep")),
        P(("blk", "rep")),
        P(("blk", "rep")),
        P("blk", None),
    )
    out_specs = (P("blk", None), P(), P(("blk", "rep"), None))
    return jax.shard_map(body, mesh=mesh, in_specs=in_specs, out_specs=out_specs, check_vma=False)
```

```python
import functools
import math

import jax
import jax.numpy as jnp
from jax import lax
from jax.experimental import pallas as pl
from jax.experimental.pallas import tpu as pltpu
from jax.sharding import PartitionSpec as P

MESH = pl.DeviceIdType.MESH
BF = jnp.bfloat16
F32 = jnp.float32
NY, NZ, NX, NC = 4, 8, 4, 2
REP = NX * NC
ROWT = 16
T = 128
COPIES = 176
FWD = (0, 7, 1, 6, 2, 5, 3, 4)
BWD = (4, 3, 5, 2, 6, 1, 7, 0)


def tables(tile_cols, tile_rows, count, metav, reqv, rqv):
    n = tile_cols.shape[1]
    across = lax.broadcasted_iota(jnp.int32, (n, n), 1)
    along = lax.broadcasted_iota(jnp.int32, (n, n), 0)
    live = count[0]

    def column(row):
        square = jnp.where(across == along, jnp.broadcast_to(row, (n, n)), 0)
        return jnp.sum(square, axis=1, keepdims=True)

    cols = tile_cols[...]
    owner, within = cols >> 4, cols & 15
    owner_c = column(owner)
    same = (owner_c == jnp.broadcast_to(owner, (n, n))) & (across < along) & (across < live)
    rank = jnp.sum(jnp.where(same, 1, 0), axis=1, keepdims=True)
    slot = column(across[:1])
    seat = jnp.where(slot < live, 2 * owner_c + rank, -1)
    hit = seat == lax.broadcasted_iota(jnp.int32, (n, T), 1)

    def spread(value):
        return jnp.sum(jnp.where(hit, value, 0), axis=0, keepdims=True)

    metav[pl.ds(0, 1), :] = spread(slot)
    metav[pl.ds(1, 1), :] = spread(column(tile_rows[...]) - ROWT) + ROWT
    asks = spread(column(within))
    reqv[...] = asks
    rqv[pl.ds(0, 1), :] = asks


def kernel(
    feats, weight, tile_values, tile_cols, tile_rows, count, cotangent,
    layer_out, grad_weight, grad_feats,
    fb0, fb1, fb2, fb3, fb4, fb5, fb6, fb7,
    values, cot, lo, metav, meta, reqv, rqv, rq,
    sy, got, prod, acc, sb, rb, fxs, fxr, mine, agg, dagg, gwa, gwy, gwz, gwr,
    bs, br, unp, blkp, sr, zs, zp, zm, xs, xr, kept,
    send_sem, recv_sem, local_sem,
):
    blk = lax.axis_index("blk")
    rep = lax.axis_index("rep")
    y, z = blk // NZ, lax.rem(blk, NZ)
    x, c = rep // NC, lax.rem(rep, NC)
    fb = (fb0, fb1, fb2, fb3, fb4, fb5, fb6, fb7)
    used = []

    def at(yy, zz, xx, cc):
        return {"blk": yy * NZ + zz, "rep": xx * NC + cc}

    def ypeer(d):
        return at(lax.rem(y + d, NY), z, x, c)

    def zpeer(d):
        return at(y, lax.rem(z + d, NZ), x, c)

    def rpeer(d):
        return {"blk": blk, "rep": lax.rem(rep + d, REP)}

    sibling = at(y, z, x, 1 - c)

    def put(src, dst, device):
        n = len(used)
        copy = pltpu.make_async_remote_copy(
            src_ref=src, dst_ref=dst, send_sem=send_sem.at[n], recv_sem=recv_sem.at[n],
            device_id=device, device_id_type=MESH,
        )
        used.append(copy)
        copy.start()
        return copy

    own = pltpu.make_async_copy(feats, fb[0], local_sem.at[0])
    load_values = pltpu.make_async_copy(tile_values, values, local_sem.at[1])
    load_cot = pltpu.make_async_copy(cotangent, cot, local_sem.at[2])
    load_meta = pltpu.make_async_copy(metav, meta, local_sem.at[3])
    load_rq = pltpu.make_async_copy(rqv, rq, local_sem.at[4])
    store_lo = pltpu.make_async_copy(lo, layer_out, local_sem.at[5])
    barrier = pltpu.get_barrier_semaphore()
    peers = (
        [ypeer(d) for d in range(1, NY)]
        + [zpeer(d) for d in range(1, NZ)]
        + [rpeer(d) for d in range(1, REP)]
    )
    for p in peers:
        pl.semaphore_signal(barrier, inc=1, device_id=p, device_id_type=MESH)
    own.start()
    load_values.start()
    load_cot.start()
    tables(tile_cols, tile_rows, count, metav, reqv, rqv)
    load_meta.start()
    pl.semaphore_wait(barrier, len(peers))

    asked = [put(reqv, rqv.at[pl.ds(NY - d, 1)], ypeer(d)) for d in range(1, NY)]

    own.wait()

    def chunk(j):
        return pl.ds(8 * c + 4 * j, 4)

    up, down = {}, {}
    for j in range(2):
        up[7, j] = put(fb[0].at[chunk(j)], fb[7].at[chunk(j)], zpeer(1))
        down[1, j] = put(fb[0].at[chunk(j)], fb[1].at[chunk(j)], zpeer(NZ - 1))
    shared = {}

    def arrive(e):
        for j in range(2):
            ring = up if e > 4 or (e == 4 and j == 0) else down
            ring[e, j].wait_recv()
            if e > 4 and (e > 5 or j == 0):
                up[e - 1, j] = put(fb[e].at[chunk(j)], fb[e - 1].at[chunk(j)], zpeer(1))
            if e < 4 and (e < 3 or j == 1):
                down[e + 1, j] = put(fb[e].at[chunk(j)], fb[e + 1].at[chunk(j)], zpeer(NZ - 1))
            shared[e, j] = put(fb[e].at[chunk(j)], fb[e].at[chunk(j)], sibling)

    def seat_of(d, e, k):
        return 2 * (lax.rem(y + d, NY) * NZ + lax.rem(z + e, NZ)) + k

    def ask_of(d, e, k):
        return rq[d, seat_of(0, e, k)] & (ROWT - 1)

    def slot_in(seat):
        return jnp.clip(meta[0, seat], 0, values.shape[0] - 1)

    sent = {}

    def pack(e):
        for d in range(1, NY):
            for k in range(2):
                sy[d - 1, e, k] = fb[e][ask_of(d, e, k)]
            sent[d, e] = put(sy.at[d - 1, e], got.at[NY - d, e], ypeer(d))
        for k in range(2):
            got[0, e, k] = fb[e][ask_of(0, e, k)]

    def spmm(e, first):
        for d in range(1, NY):
            sent[d, e].wait_recv()
        rows = []
        for d in range(NY):
            for k in range(2):
                seat = seat_of(d, e, k)
                prod[2 * d + k] = jnp.dot(
                    values[slot_in(seat)], got[d, e, k], preferred_element_type=F32
                )
                rows.append(meta[1, seat])

        def add(t, carry):
            total = jnp.zeros((T, T), F32) if first else acc[t]
            for i in range(2 * NY):
                total = total + prod[i] * jnp.where(rows[i] == t, 1.0, 0.0).astype(F32)
            acc[t] = total
            return carry

        lax.fori_loop(0, ROWT, add, 0)

    for i, e in enumerate(FWD):
        if e:
            arrive(e)
            if i >= 2:
                spmm(FWD[i - 2], i == 2)
            for j in range(2):
                shared[e, j].wait_recv()
        else:
            for copy in asked:
                copy.wait_recv()
            load_rq.start()
            load_meta.wait()
            load_values.wait()
            load_rq.wait()
        pack(e)
    spmm(FWD[-2], False)
    spmm(FWD[-1], False)

    def home_tile(there, j):
        return 4 * there + 2 * c + j

    def other_tile(there, j):
        return 4 * there + 2 * (1 - c) + j

    order = [lax.rem(x + d, NX) for d in (2, 1, 3, 0)]
    halves = []
    for q, there in enumerate(order):
        for j in range(2):
            sb[q, j] = acc[other_tile(there, j)].astype(BF)
        halves.append(put(sb.at[q], rb.at[q], sibling))
    scattered = {}
    for q, there in enumerate(order):
        halves[q].wait_recv()
        for j in range(2):
            total = acc[home_tile(there, j)] + rb[q, j].astype(F32)
            if q < 3:
                fxs[q, j] = total.astype(BF)
            else:
                mine[j] = total
        if q < 3:
            d = (2, 1, 3)[q]
            scattered[d] = put(fxs.at[q], fxr.at[NX - d], at(y, z, there, c))
    for d in (1, 3, 2):
        scattered[NX - d].wait_recv()
        for j in range(2):
            mine[j] += fxr[d, j].astype(F32)
    own_pair = pl.ds(2 * rep, 2)
    own_rows = pl.ds(pl.multiple_of(256 * rep, 256), 256)

    def slope(a, cots):
        pre = jnp.dot(a, weight[...], preferred_element_type=F32)
        sig = jax.nn.sigmoid(pre)
        dpre = (cots.astype(F32) * sig * (1.0 + pre * (1.0 - sig))).astype(BF)
        return pre, sig, dpre

    load_cot.wait()
    agg[own_pair] = mine[...].astype(BF)
    _, _, dpre_own = slope(mine[...].astype(BF).reshape(256, T), cot[own_rows, :])
    back = lax.dot_general(dpre_own, weight[...], (((1,), (1,)), ((), ())), preferred_element_type=F32)
    dagg[own_pair] = back.astype(BF).reshape(2, T, T)

    def pair_of(xx, cc):
        return pl.ds(2 * (2 * xx + cc), 2)

    gathered = {d: put(dagg.at[own_pair], dagg.at[own_pair], at(y, z, lax.rem(x + d, NX), c)) for d in (2, 1, 3)}
    passed = [put(dagg.at[own_pair], dagg.at[own_pair], sibling)]
    for d in (1, 3, 2):
        gathered[d].wait_recv()
        piece = dagg.at[pair_of(lax.rem(x + NX - d, NX), c)]
        passed.append(put(piece, piece, sibling))
    for copy in passed:
        copy.wait_recv()
    agg_all = [put(agg.at[own_pair], agg.at[own_pair], rpeer(d)) for d in range(1, REP)]

    gwa[...] = jnp.zeros_like(gwa)

    def dense(i, carry):
        rows = pl.ds(pl.multiple_of(i * 256, 256), 256)
        a = agg[pl.ds(2 * i, 2)].reshape(256, T)
        pre, sig, dpre = slope(a, cot[rows, :])
        lo[rows, :] = (pre * sig).astype(BF)
        gwa[...] += lax.dot_general(a, dpre, (((0,), (0,)), ((), ())), preferred_element_type=F32)
        return carry

    strip = pl.ds(pl.multiple_of(16 * rep, 16), 16)
    gw_y = []

    def gw_first():
        gwy[pl.ds(y, 1)] = (gwa[strip, :] * (1.0 / 256.0))[None]
        for d in range(1, NY):
            gw_y.append(put(gwy.at[pl.ds(y, 1)], gwy.at[pl.ds(y, 1)], ypeer(d)))

    back_sent = {}

    def products(e):
        for d in (1, 2, 3, 0):
            for k in range(2):
                seat = seat_of(d, e, k)
                row = meta[1, seat]
                live = jnp.where(row < ROWT, 1.0, 0.0).astype(F32)
                out = lax.dot_general(
                    values[slot_in(seat)], dagg[row & (ROWT - 1)],
                    (((0,), (0,)), ((), ())), preferred_element_type=F32,
                )
                if d:
                    bs[d - 1, e, k] = (out * live).astype(BF)
                else:
                    br[0, e, k] = (out * live).astype(BF)
            if d:
                back_sent[d, e] = put(bs.at[d - 1, e], br.at[NY - d, e], ypeer(d))

    sib_sent = {}

    def place(t):
        return 8 * lax.rem(t // 2, 2) + 2 * (t // 4) + lax.rem(t, 2)

    def collect(e):
        ids = []
        for d in range(NY):
            if d:
                back_sent[NY - d, e].wait_recv()
            for k in range(2):
                unp[2 * d + k] = br[d, e, k].astype(F32)
                ids.append(place(ask_of(d, e, k)))

        def add(t, carry):
            total = jnp.zeros((T, T), F32)
            for i in range(2 * NY):
                total = total + unp[i] * jnp.where(ids[i] == t, 1.0, 0.0).astype(F32)
            blkp[e, t] = total.astype(BF)
            return carry

        lax.fori_loop(0, ROWT, add, 0)
        sib_sent[e] = put(blkp.at[e, pl.ds(8 * (1 - c), 8)], sr.at[e], sibling)

    x_sent = {}

    def across(e):
        sib_sent[e].wait_recv()
        for d in (2, 1, 3, 0):
            there = lax.rem(x + d, NX)
            for j in range(2):
                total = blkp[e, 8 * c + 2 * there + j].astype(F32) + sr[e, 2 * there + j].astype(F32)
                if d:
                    xs[e, d - 1, j] = total.astype(BF)
                else:
                    kept[e, j] = total
            if d:
                x_sent[d, e] = put(xs.at[e, d - 1], xr.at[e, NX - d], at(y, z, there, c))

    zup, zdown = {}, {}

    def chain(e):
        for d in range(1, NX):
            x_sent[d, e].wait_recv()
        for j in range(2):
            total = kept[e, j]
            for d in range(1, NX):
                total = total + xr[e, d, j].astype(F32)
            if e == 0:
                zup[0, j].wait_recv()
                zdown[0, j].wait_recv()
                total = total + zp[0, j].astype(F32) + zm[0, j].astype(F32)
                grad_feats[pl.ds(T * j, T), :] = total
                continue
            rising = e < 4 or (e == 4 and j == 0)
            begins = e == 4 or (e == 3 and j == 1) or (e == 5 and j == 0)
            if not begins:
                (zup if rising else zdown)[e, j].wait_recv()
                total = total + (zp if rising else zm)[e, j].astype(F32)
            zs[e, j] = total.astype(BF)
            if rising:
                zup[e - 1, j] = put(zs.at[e, j], zp.at[e - 1, j], zpeer(1))
            else:
                zdown[(e + 1) % 8, j] = put(zs.at[e, j], zm.at[(e + 1) % 8, j], zpeer(NZ - 1))

    gw_z, gw_r = [], []

    def gw_second():
        for copy in gw_y:
            copy.wait_recv()
        gwz[pl.ds(z, 1)] = (gwy[0] + gwy[1] + gwy[2] + gwy[3])[None]
        for d in range(1, NZ):
            gw_z.append(put(gwz.at[pl.ds(z, 1)], gwz.at[pl.ds(z, 1)], zpeer(d)))

    def gw_third():
        for copy in gw_z:
            copy.wait_recv()
        total = gwz[0]
        for i in range(1, NZ):
            total = total + gwz[i]
        gwr[strip, :] = total
        for d in range(1, REP):
            gw_r.append(put(gwr.at[strip], gwr.at[strip], rpeer(d)))

    lead = 3
    for i in range(lead):
        products(BWD[i])
    n = len(BWD)
    for i in range(n):
        collect(BWD[i])
        if i + lead < n:
            products(BWD[i + lead])
        if i == 0:
            for copy in agg_all:
                copy.wait_recv()
        if i < 4:
            lax.fori_loop(2 * i, 2 * i + 2, dense, 0)
        across(BWD[i])
        if i:
            chain(BWD[i - 1])
        if i == 3:
            store_lo.start()
            gw_first()
        if i == 4:
            gw_second()
        if i == 6:
            gw_third()
    chain(BWD[-1])

    for copy in gw_r:
        copy.wait_recv()
    grad_weight[...] = gwr[...]
    store_lo.wait()
    for copy in used:
        copy.wait_send()


def finish(lo, gw, gf, lo_out, gw_out, gf_out, lo_v, gw_v, gf_v, sems):
    parts = [(lo.at[pl.ds(512 * i, 512)], lo_v.at[pl.ds(512 * i, 512)], lo_out.at[pl.ds(512 * i, 512)]) for i in range(4)]
    parts += [(gw, gw_v, gw_out), (gf, gf_v, gf_out)]
    loads = [pltpu.make_async_copy(a, v, sems.at[0, i]) for i, (a, v, _) in enumerate(parts)]
    stores = [pltpu.make_async_copy(v, o, sems.at[1, i]) for i, (_, v, o) in enumerate(parts)]
    for copy in loads:
        copy.start()
    for load, store in zip(loads, stores):
        load.wait()
        store.start()
    for copy in stores:
        copy.wait()


def body(node_feats, weight, tile_values, tile_rows, tile_cols, tile_count, cotangent):
    slots = tile_values.shape[0]
    vmem = pl.BlockSpec(memory_space=pltpu.VMEM)
    smem = pl.BlockSpec(memory_space=pltpu.SMEM)
    hbm = pl.BlockSpec(memory_space=pl.ANY)
    ints = lambda space, n: space((n, T), jnp.int32)
    tiles = lambda *lead: pltpu.VMEM((*lead, T, T), BF)
    wide = lambda *lead: pltpu.VMEM((*lead, T, T), F32)
    outs = pl.pallas_call(
        kernel,
        out_shape=(
            jax.ShapeDtypeStruct((2048, 256), BF),
            jax.ShapeDtypeStruct((128, 256), F32),
            jax.ShapeDtypeStruct((256, 128), F32),
        ),
        in_specs=[hbm, vmem, hbm, vmem, vmem, smem, hbm],
        out_specs=(hbm, vmem, vmem),
        scratch_shapes=[tiles(ROWT) for _ in range(8)] + [
            tiles(slots), pltpu.VMEM((2048, 256), BF), pltpu.VMEM((2048, 256), BF),
            ints(pltpu.VMEM, 2), ints(pltpu.SMEM, 2), ints(pltpu.VMEM, 1),
            ints(pltpu.VMEM, 4), ints(pltpu.SMEM, 4),
            tiles(3, 8, 2), tiles(4, 8, 2), wide(8), wide(16),
            tiles(4, 2), tiles(4, 2), tiles(3, 2), tiles(4, 2), wide(2), tiles(16), tiles(16),
            pltpu.VMEM((128, 256), F32), pltpu.VMEM((NY, 16, 256), F32),
            pltpu.VMEM((NZ, 16, 256), F32), pltpu.VMEM((128, 256), F32),
            tiles(3, 8, 2), tiles(4, 8, 2), wide(8), tiles(8, 16), tiles(8, 8),
            tiles(8, 2), tiles(8, 2), tiles(8, 2), tiles(8, 3, 2), tiles(8, 4, 2), wide(8, 2),
            pltpu.SemaphoreType.DMA((COPIES,)), pltpu.SemaphoreType.DMA((COPIES,)),
            pltpu.SemaphoreType.DMA((6,)),
        ],
        compiler_params=pltpu.CompilerParams(
            collective_id=1, has_side_effects=True, vmem_limit_bytes=56 << 20
        ),
        name="layer",
    )(node_feats.reshape(ROWT, T, T), weight, tile_values,
      tile_cols.reshape(1, slots), tile_rows.reshape(1, slots), tile_count, cotangent)
    return pl.pallas_call(
        finish,
        out_shape=tuple(jax.ShapeDtypeStruct(o.shape, o.dtype) for o in outs),
        in_specs=[hbm] * 3,
        out_specs=(hbm,) * 3,
        scratch_shapes=[pltpu.VMEM(o.shape, o.dtype) for o in outs] + [pltpu.SemaphoreType.DMA((2, 6))],
        name="finish",
    )(*outs)


def solution(mesh):
    in_specs = (
        P("blk", None),
        P(),
        P(("blk", "rep"), None, None),
        P(("blk", "rep")),
        P(("blk", "rep")),
        P(("blk", "rep")),
        P("blk", None),
    )
    out_specs = (P("blk", None), P(), P(("blk", "rep"), None))
    return jax.shard_map(body, mesh=mesh, in_specs=in_specs, out_specs=out_specs, check_vma=False)
```

```python
import functools
import math

import jax
import jax.numpy as jnp
from jax import lax
from jax.experimental import pallas as pl
from jax.experimental.pallas import tpu as pltpu
from jax.sharding import PartitionSpec as P

MESH = pl.DeviceIdType.MESH
BF = jnp.bfloat16
F32 = jnp.float32
NY, NZ, NX, NC = 4, 8, 4, 2
REP = NX * NC
ROWT = 16
T = 128
COPIES = 176
BWD = (4, 3, 5, 2, 6, 1, 7, 0)


def tables(tile_cols, tile_rows, count, metav, reqv, rqv):
    n = tile_cols.shape[1]
    across = lax.broadcasted_iota(jnp.int32, (n, n), 1)
    along = lax.broadcasted_iota(jnp.int32, (n, n), 0)
    live = count[0]

    def column(row):
        square = jnp.where(across == along, jnp.broadcast_to(row, (n, n)), 0)
        return jnp.sum(square, axis=1, keepdims=True)

    cols = tile_cols[...]
    owner, within = cols >> 4, cols & 15
    owner_c = column(owner)
    same = (owner_c == jnp.broadcast_to(owner, (n, n))) & (across < along) & (across < live)
    rank = jnp.sum(jnp.where(same, 1, 0), axis=1, keepdims=True)
    slot = column(across[:1])
    seat = jnp.where(slot < live, 2 * owner_c + rank, -1)
    hit = seat == lax.broadcasted_iota(jnp.int32, (n, T), 1)

    def spread(value):
        return jnp.sum(jnp.where(hit, value, 0), axis=0, keepdims=True)

    metav[pl.ds(0, 1), :] = spread(slot)
    metav[pl.ds(1, 1), :] = spread(column(tile_rows[...]) - ROWT) + ROWT
    asks = spread(column(within))
    reqv[...] = asks
    rqv[pl.ds(0, 1), :] = asks


def kernel(
    feats, weight, tile_values, tile_cols, tile_rows, count, cotangent,
    layer_out, grad_weight, grad_feats,
    fb0, fb1, fb2, fb3, fb4, fb5, fb6, fb7,
    values, cot, lo, metav, meta, reqv, rqv, rq,
    sy, got, prod, acc, sb, rb, fxs, fxr, mine, agg, dagg, gwa, gwy, gwz, gwr,
    bs, br, unp, blkp, sr, zs, zp, zm, xs, xr, kept,
    send_sem, recv_sem, local_sem,
):
    blk = lax.axis_index("blk")
    rep = lax.axis_index("rep")
    y, z = blk // NZ, lax.rem(blk, NZ)
    x, c = rep // NC, lax.rem(rep, NC)
    fb = (fb0, fb1, fb2, fb3, fb4, fb5, fb6, fb7)
    used = []

    def at(yy, zz, xx, cc):
        return {"blk": yy * NZ + zz, "rep": xx * NC + cc}

    def ypeer(d):
        return at(lax.rem(y + d, NY), z, x, c)

    def zpeer(d):
        return at(y, lax.rem(z + d, NZ), x, c)

    def rpeer(d):
        return {"blk": blk, "rep": lax.rem(rep + d, REP)}

    sibling = at(y, z, x, 1 - c)

    def put(src, dst, device):
        n = len(used)
        copy = pltpu.make_async_remote_copy(
            src_ref=src, dst_ref=dst, send_sem=send_sem.at[n], recv_sem=recv_sem.at[n],
            device_id=device, device_id_type=MESH,
        )
        used.append(copy)
        copy.start()
        return copy

    own = pltpu.make_async_copy(feats, fb[0], local_sem.at[0])
    load_values = pltpu.make_async_copy(tile_values, values, local_sem.at[1])
    load_cot = pltpu.make_async_copy(cotangent, cot, local_sem.at[2])
    load_meta = pltpu.make_async_copy(metav, meta, local_sem.at[3])
    load_rq = pltpu.make_async_copy(rqv, rq, local_sem.at[4])
    store_lo = pltpu.make_async_copy(lo, layer_out, local_sem.at[5])
    barrier = pltpu.get_barrier_semaphore()
    peers = (
        [ypeer(d) for d in range(1, NY)]
        + [zpeer(d) for d in range(1, NZ)]
        + [rpeer(d) for d in range(1, REP)]
    )
    for p in peers:
        pl.semaphore_signal(barrier, inc=1, device_id=p, device_id_type=MESH)
    own.start()
    load_values.start()
    load_cot.start()
    tables(tile_cols, tile_rows, count, metav, reqv, rqv)
    load_meta.start()
    pl.semaphore_wait(barrier, len(peers))

    asked = [put(reqv, rqv.at[pl.ds(NY - d, 1)], ypeer(d)) for d in range(1, NY)]

    own.wait()

    def chunk(j):
        return pl.ds(8 * c + 4 * j, 4)

    up, down = {}, {}
    for j in range(2):
        up[7, j] = put(fb[0].at[chunk(j)], fb[7].at[chunk(j)], zpeer(1))
        down[1, j] = put(fb[0].at[chunk(j)], fb[1].at[chunk(j)], zpeer(NZ - 1))
    shared = {}

    def arrive(e):
        for j in range(2):
            ring = up if e > 4 or (e == 4 and j == 0) else down
            ring[e, j].wait_recv()
            if e > 4 and (e > 5 or j == 0):
                up[e - 1, j] = put(fb[e].at[chunk(j)], fb[e - 1].at[chunk(j)], zpeer(1))
            if e < 4 and (e < 3 or j == 1):
                down[e + 1, j] = put(fb[e].at[chunk(j)], fb[e + 1].at[chunk(j)], zpeer(NZ - 1))
            shared[e, j] = put(fb[e].at[chunk(j)], fb[e].at[chunk(j)], sibling)

    def seat_of(d, e, k):
        return 2 * (lax.rem(y + d, NY) * NZ + lax.rem(z + e, NZ)) + k

    def ask_of(d, e, k):
        return rq[d, seat_of(0, e, k)] & (ROWT - 1)

    def slot_in(seat):
        return jnp.clip(meta[0, seat], 0, values.shape[0] - 1)

    sent = {}

    def pack(e):
        for d in range(1, NY):
            for k in range(2):
                sy[d - 1, e, k] = fb[e][ask_of(d, e, k)]
            sent[d, e] = put(sy.at[d - 1, e], got.at[NY - d, e], ypeer(d))
        for k in range(2):
            got[0, e, k] = fb[e][ask_of(0, e, k)]

    def spmm(e, first):
        for d in range(1, NY):
            sent[d, e].wait_recv()
        rows = []
        for d in range(NY):
            for k in range(2):
                seat = seat_of(d, e, k)
                prod[2 * d + k] = jnp.dot(
                    values[slot_in(seat)], got[d, e, k], preferred_element_type=F32
                )
                rows.append(meta[1, seat])

        def add(t, carry):
            total = jnp.zeros((T, T), F32) if first else acc[t]
            for i in range(2 * NY):
                total = total + prod[i] * jnp.where(rows[i] == t, 1.0, 0.0).astype(F32)
            acc[t] = total
            return carry

        lax.fori_loop(0, ROWT, add, 0)

    def finish_block(e):
        for j in range(2):
            shared[e, j].wait_recv()
        pack(e)

    for copy in asked:
        copy.wait_recv()
    load_rq.start()
    load_meta.wait()
    load_values.wait()
    load_rq.wait()
    pack(0)
    for near, far, ready in ((7, 1, ()), (6, 2, (0,)), (5, 3, (7,))):
        arrive(near)
        arrive(far)
        finish_block(near)
        finish_block(far)
        for e in ready:
            spmm(e, e == 0)
    arrive(4)
    finish_block(4)
    for e in (1, 6, 2, 5, 3, 4):
        spmm(e, False)

    def home_tile(there, j):
        return 4 * there + 2 * c + j

    def other_tile(there, j):
        return 4 * there + 2 * (1 - c) + j

    order = [lax.rem(x + d, NX) for d in (2, 1, 3, 0)]
    halves = []
    for q, there in enumerate(order):
        for j in range(2):
            sb[q, j] = acc[other_tile(there, j)].astype(BF)
        halves.append(put(sb.at[q], rb.at[q], sibling))
    scattered = {}
    for q, there in enumerate(order):
        halves[q].wait_recv()
        for j in range(2):
            total = acc[home_tile(there, j)] + rb[q, j].astype(F32)
            if q < 3:
                fxs[q, j] = total.astype(BF)
            else:
                mine[j] = total
        if q < 3:
            d = (2, 1, 3)[q]
            scattered[d] = put(fxs.at[q], fxr.at[NX - d], at(y, z, there, c))
    for d in (1, 3, 2):
        scattered[NX - d].wait_recv()
        for j in range(2):
            mine[j] += fxr[d, j].astype(F32)
    own_pair = pl.ds(2 * rep, 2)
    own_rows = pl.ds(pl.multiple_of(256 * rep, 256), 256)

    def slope(a, cots):
        pre = jnp.dot(a, weight[...], preferred_element_type=F32)
        sig = jax.nn.sigmoid(pre)
        dpre = (cots.astype(F32) * sig * (1.0 + pre * (1.0 - sig))).astype(BF)
        return pre, sig, dpre

    load_cot.wait()
    agg[own_pair] = mine[...].astype(BF)
    _, _, dpre_own = slope(mine[...].astype(BF).reshape(256, T), cot[own_rows, :])
    back = lax.dot_general(dpre_own, weight[...], (((1,), (1,)), ((), ())), preferred_element_type=F32)
    dagg[own_pair] = back.astype(BF).reshape(2, T, T)

    def pair_of(xx, cc):
        return pl.ds(2 * (2 * xx + cc), 2)

    gathered = {d: put(dagg.at[own_pair], dagg.at[own_pair], at(y, z, lax.rem(x + d, NX), c)) for d in (2, 1, 3)}
    passed = [put(dagg.at[own_pair], dagg.at[own_pair], sibling)]
    for d in (1, 3, 2):
        gathered[d].wait_recv()
        piece = dagg.at[pair_of(lax.rem(x + NX - d, NX), c)]
        passed.append(put(piece, piece, sibling))
    for copy in passed:
        copy.wait_recv()
    agg_all = [put(agg.at[own_pair], agg.at[own_pair], rpeer(d)) for d in range(1, REP)]

    gwa[...] = jnp.zeros_like(gwa)

    def dense(i, carry):
        rows = pl.ds(pl.multiple_of(i * 256, 256), 256)
        a = agg[pl.ds(2 * i, 2)].reshape(256, T)
        pre, sig, dpre = slope(a, cot[rows, :])
        lo[rows, :] = (pre * sig).astype(BF)
        gwa[...] += lax.dot_general(a, dpre, (((0,), (0,)), ((), ())), preferred_element_type=F32)
        return carry

    strip = pl.ds(pl.multiple_of(16 * rep, 16), 16)
    gw_y = []

    def gw_first():
        gwy[pl.ds(y, 1)] = (gwa[strip, :] * (1.0 / 256.0))[None]
        for d in range(1, NY):
            gw_y.append(put(gwy.at[pl.ds(y, 1)], gwy.at[pl.ds(y, 1)], ypeer(d)))

    back_sent = {}

    def products(e):
        for d in (1, 2, 3, 0):
            for k in range(2):
                seat = seat_of(d, e, k)
                row = meta[1, seat]
                live = jnp.where(row < ROWT, 1.0, 0.0).astype(F32)
                out = lax.dot_general(
                    values[slot_in(seat)], dagg[row & (ROWT - 1)],
                    (((0,), (0,)), ((), ())), preferred_element_type=F32,
                )
                if d:
                    bs[d - 1, e, k] = (out * live).astype(BF)
                else:
                    br[0, e, k] = (out * live).astype(BF)
            if d:
                back_sent[d, e] = put(bs.at[d - 1, e], br.at[NY - d, e], ypeer(d))

    sib_sent = {}

    def place(t):
        return 8 * lax.rem(t // 2, 2) + 2 * (t // 4) + lax.rem(t, 2)

    def collect(e):
        ids = []
        for d in range(NY):
            if d:
                back_sent[NY - d, e].wait_recv()
            for k in range(2):
                unp[2 * d + k] = br[d, e, k].astype(F32)
                ids.append(place(ask_of(d, e, k)))

        def add(t, carry):
            total = jnp.zeros((T, T), F32)
            for i in range(2 * NY):
                total = total + unp[i] * jnp.where(ids[i] == t, 1.0, 0.0).astype(F32)
            blkp[e, t] = total.astype(BF)
            return carry

        lax.fori_loop(0, ROWT, add, 0)
        sib_sent[e] = put(blkp.at[e, pl.ds(8 * (1 - c), 8)], sr.at[e], sibling)

    x_sent = {}

    def across(e):
        sib_sent[e].wait_recv()
        for d in (2, 1, 3, 0):
            there = lax.rem(x + d, NX)
            for j in range(2):
                total = blkp[e, 8 * c + 2 * there + j].astype(F32) + sr[e, 2 * there + j].astype(F32)
                if d:
                    xs[e, d - 1, j] = total.astype(BF)
                else:
                    kept[e, j] = total
            if d:
                x_sent[d, e] = put(xs.at[e, d - 1], xr.at[e, NX - d], at(y, z, there, c))

    zup, zdown = {}, {}

    def chain(e):
        for d in range(1, NX):
            x_sent[d, e].wait_recv()
        for j in range(2):
            total = kept[e, j]
            for d in range(1, NX):
                total = total + xr[e, d, j].astype(F32)
            if e == 0:
                zup[0, j].wait_recv()
                zdown[0, j].wait_recv()
                total = total + zp[0, j].astype(F32) + zm[0, j].astype(F32)
                grad_feats[pl.ds(T * j, T), :] = total
                continue
            rising = e < 4 or (e == 4 and j == 0)
            begins = e == 4 or (e == 3 and j == 1) or (e == 5 and j == 0)
            if not begins:
                (zup if rising else zdown)[e, j].wait_recv()
                total = total + (zp if rising else zm)[e, j].astype(F32)
            zs[e, j] = total.astype(BF)
            if rising:
                zup[e - 1, j] = put(zs.at[e, j], zp.at[e - 1, j], zpeer(1))
            else:
                zdown[(e + 1) % 8, j] = put(zs.at[e, j], zm.at[(e + 1) % 8, j], zpeer(NZ - 1))

    gw_z, gw_r = [], []

    def gw_second():
        for copy in gw_y:
            copy.wait_recv()
        gwz[pl.ds(z, 1)] = (gwy[0] + gwy[1] + gwy[2] + gwy[3])[None]
        for d in range(1, NZ):
            gw_z.append(put(gwz.at[pl.ds(z, 1)], gwz.at[pl.ds(z, 1)], zpeer(d)))

    def gw_third():
        for copy in gw_z:
            copy.wait_recv()
        total = gwz[0]
        for i in range(1, NZ):
            total = total + gwz[i]
        gwr[strip, :] = total
        for d in range(1, REP):
            gw_r.append(put(gwr.at[strip], gwr.at[strip], rpeer(d)))

    lead = 3
    for i in range(lead):
        products(BWD[i])
    n = len(BWD)
    for i in range(n):
        collect(BWD[i])
        if i + lead < n:
            products(BWD[i + lead])
        if i == 0:
            for copy in agg_all:
                copy.wait_recv()
        if i < 4:
            lax.fori_loop(2 * i, 2 * i + 2, dense, 0)
        across(BWD[i])
        if i:
            chain(BWD[i - 1])
        if i == 3:
            store_lo.start()
            gw_first()
        if i == 4:
            gw_second()
        if i == 6:
            gw_third()
    chain(BWD[-1])

    for copy in gw_r:
        copy.wait_recv()
    grad_weight[...] = gwr[...]
    store_lo.wait()
    for copy in used:
        copy.wait_send()


def finish(lo, gw, gf, lo_out, gw_out, gf_out, lo_v, gw_v, gf_v, sems):
    parts = [(lo.at[pl.ds(512 * i, 512)], lo_v.at[pl.ds(512 * i, 512)], lo_out.at[pl.ds(512 * i, 512)]) for i in range(4)]
    parts += [(gw, gw_v, gw_out), (gf, gf_v, gf_out)]
    loads = [pltpu.make_async_copy(a, v, sems.at[0, i]) for i, (a, v, _) in enumerate(parts)]
    stores = [pltpu.make_async_copy(v, o, sems.at[1, i]) for i, (_, v, o) in enumerate(parts)]
    for copy in loads:
        copy.start()
    for load, store in zip(loads, stores):
        load.wait()
        store.start()
    for copy in stores:
        copy.wait()


def body(node_feats, weight, tile_values, tile_rows, tile_cols, tile_count, cotangent):
    slots = tile_values.shape[0]
    vmem = pl.BlockSpec(memory_space=pltpu.VMEM)
    smem = pl.BlockSpec(memory_space=pltpu.SMEM)
    hbm = pl.BlockSpec(memory_space=pl.ANY)
    ints = lambda space, n: space((n, T), jnp.int32)
    tiles = lambda *lead: pltpu.VMEM((*lead, T, T), BF)
    wide = lambda *lead: pltpu.VMEM((*lead, T, T), F32)
    outs = pl.pallas_call(
        kernel,
        out_shape=(
            jax.ShapeDtypeStruct((2048, 256), BF),
            jax.ShapeDtypeStruct((128, 256), F32),
            jax.ShapeDtypeStruct((256, 128), F32),
        ),
        in_specs=[hbm, vmem, hbm, vmem, vmem, smem, hbm],
        out_specs=(hbm, vmem, vmem),
        scratch_shapes=[tiles(ROWT) for _ in range(8)] + [
            tiles(slots), pltpu.VMEM((2048, 256), BF), pltpu.VMEM((2048, 256), BF),
            ints(pltpu.VMEM, 2), ints(pltpu.SMEM, 2), ints(pltpu.VMEM, 1),
            ints(pltpu.VMEM, 4), ints(pltpu.SMEM, 4),
            tiles(3, 8, 2), tiles(4, 8, 2), wide(8), wide(16),
            tiles(4, 2), tiles(4, 2), tiles(3, 2), tiles(4, 2), wide(2), tiles(16), tiles(16),
            pltpu.VMEM((128, 256), F32), pltpu.VMEM((NY, 16, 256), F32),
            pltpu.VMEM((NZ, 16, 256), F32), pltpu.VMEM((128, 256), F32),
            tiles(3, 8, 2), tiles(4, 8, 2), wide(8), tiles(8, 16), tiles(8, 8),
            tiles(8, 2), tiles(8, 2), tiles(8, 2), tiles(8, 3, 2), tiles(8, 4, 2), wide(8, 2),
            pltpu.SemaphoreType.DMA((COPIES,)), pltpu.SemaphoreType.DMA((COPIES,)),
            pltpu.SemaphoreType.DMA((6,)),
        ],
        compiler_params=pltpu.CompilerParams(
            collective_id=1, has_side_effects=True, vmem_limit_bytes=56 << 20
        ),
        name="layer",
    )(node_feats.reshape(ROWT, T, T), weight, tile_values,
      tile_cols.reshape(1, slots), tile_rows.reshape(1, slots), tile_count, cotangent)
    return pl.pallas_call(
        finish,
        out_shape=tuple(jax.ShapeDtypeStruct(o.shape, o.dtype) for o in outs),
        in_specs=[hbm] * 3,
        out_specs=(hbm,) * 3,
        scratch_shapes=[pltpu.VMEM(o.shape, o.dtype) for o in outs] + [pltpu.SemaphoreType.DMA((2, 6))],
        name="finish",
    )(*outs)


def solution(mesh):
    in_specs = (
        P("blk", None),
        P(),
        P(("blk", "rep"), None, None),
        P(("blk", "rep")),
        P(("blk", "rep")),
        P(("blk", "rep")),
        P("blk", None),
    )
    out_specs = (P("blk", None), P(), P(("blk", "rep"), None))
    return jax.shard_map(body, mesh=mesh, in_specs=in_specs, out_specs=out_specs, check_vma=False)
```
